256 devices in a mesh: ctx: 16 (over z, x_hi), head: 4 (over x_lo, core), doc: 4 (over y).
Axes of the slice: x: 4 (x_hi: 2, x_lo: 2; x = x_hi * 2 + x_lo), y: 4, z: 8, core: 2. Of those that a mesh axis runs over, the one named last changes fastest.
Arguments:
- queries: bfloat16 [16384, 8192], P(('doc', 'ctx'), 'head'), parts along dimension 0, may hold values from -80 to 80
- keys: bfloat16 [16384, 1024], P(('doc', 'ctx'), 'head'), parts along dimension 0, may hold values from -4 to 4
- values: bfloat16 [16384, 1024], P(('doc', 'ctx'), 'head'), parts along dimension 0, may hold values from -6 to 6
- image_keys: bfloat16 [32768, 1024], P(('doc', 'ctx'), 'head'), parts along dimension 0, may hold values from -24 to 24
- image_values: bfloat16 [32768, 1024], P(('doc', 'ctx'), 'head'), parts along dimension 0, may hold values from -6 to 6
- cross_lo: int32 [16384], P(('doc', 'ctx')), parts along dimension 0, may hold values from 0 to 4096, as said below
- cross_hi: int32 [16384], P(('doc', 'ctx')), parts along dimension 0, may hold values from 0 to 8192, as said below
- query_gain: float32 [128], replicated, may hold values from 0.5 to 2
- cross_gate: float32 [64], P('head'), may hold values from -1.5 to 1.5
Outputs:
- self_heads: bfloat16 [16384, 8192], P(('doc', 'ctx'), 'head'), parts along dimension 0
- cross_heads: bfloat16 [16384, 8192], P(('doc', 'ctx'), 'head'), parts along dimension 0
The draws below stay inside these ranges and needn't reach their ends.
There are 4 independent parts, one for each index of `doc`. The reference program is written for one: setup_inputs(seed, part) draws one part's arguments, and reference() takes and returns one part's arrays. A program takes and returns all parts, laid end to end along the dimension named above; an argument that names none is the same for every part. Nothing has to cross between parts.
Inputs may be any that keep to these rules, and one draw needn't show every extreme that they name: `cross_lo`: images sit at distinct token positions after the first token. A token's range covers whole images of 2048 tokens: it ends after the last image placed at or before the token and begins at most two images before that end; tokens before the first image have an empty range. cross_hi[t] >= cross_lo[t], a multiple of 2048, never falling along the document.
All inputs are finite; a program needn't handle non-finite values.
Results may differ from the reference program's by a relative error of at most 0.018.
Values may be sent and summed in bfloat16 or wider, within the bound.
A program may use at most 64 MiB of HBM per device.

```python
import math
import jax
import jax.numpy as jnp
from jax import lax

H = 64
KVH = 8
HD = 128
NIMG = 4
TOKENS = 4096
IMG = 2048


def base_keys(key):
    return jnp.clip(jax.random.normal(key, (TOKENS, KVH * HD), jnp.float32), -4.0, 4.0)


def draw_keys(key, part):
    shared = base_keys(key)
    return shared.astype(jnp.bfloat16)


def draw_queries(key, part):
    own_key = jax.random.fold_in(key, 12)
    drawn = jnp.clip(jax.random.normal(own_key, (TOKENS, H * HD), jnp.float32), -4.0, 4.0)
    return drawn.astype(jnp.bfloat16)


def draw_values(key, part):
    own_key = jax.random.fold_in(key, 13)
    drawn = jax.random.normal(own_key, (TOKENS, KVH * HD), jnp.float32)
    return jnp.clip(drawn, -6.0, 6.0).astype(jnp.bfloat16)


def draw_image_keys(key, part):
    own_key = jax.random.fold_in(key, 14)
    drawn = jnp.clip(jax.random.normal(own_key, (NIMG * IMG, KVH * HD), jnp.float32), -6.0, 6.0)
    return drawn.astype(jnp.bfloat16)


def seen_images(key):
    picked = jax.random.permutation(key, TOKENS - 1)[:NIMG].astype(jnp.int32) + 1
    places = jnp.sort(picked)
    token_rows = jnp.arange(TOKENS, dtype=jnp.int32)
    return jnp.sum((places[None, :] <= token_rows[:, None]).astype(jnp.int32), axis=1)


def draw_cross_lo(key, part):
    seen = seen_images(key)
    return (jnp.maximum(seen - 2, 0) * IMG).astype(jnp.int32)


def draw_cross_hi(key, part):
    seen = seen_images(key)
    return (seen * IMG).astype(jnp.int32)


def levels(rng, shape, split, low, top_value):
    level, own = 1.0, jax.random.fold_in(rng, 6)
    for dim, parts in split:
        steps = jnp.exp(jax.random.uniform(jax.random.fold_in(own, dim), (parts,), jnp.float32, low / len(split), top_value / len(split)))
        level = level * jnp.repeat(steps, shape[dim] // parts).reshape([-1 if axis == dim else 1 for axis in range(len(shape))])
    return level


def noise(rng, dims, deviation, bound, shards=(), kind=jnp.bfloat16):
    factor_of = levels(rng, dims, shards, -0.22, 0.18) if shards else 1.0
    array = jax.random.normal(rng, dims, jnp.float32) * deviation * factor_of
    return jnp.minimum(jnp.maximum(array, -bound), bound).astype(kind)


def setup_inputs(seed: int = 0, part: int = 0) -> dict:
    key_of = jax.random.split(jax.random.key(seed), 10)
    part_keys = jax.random.split(jax.random.fold_in(key_of[9], part), 10)
    return {
        "queries": draw_queries(jax.random.fold_in(jax.random.fold_in(key_of[9], part), 71), part),
        "keys": draw_keys(jax.random.fold_in(jax.random.fold_in(key_of[9], part), 71), part),
        "values": draw_values(jax.random.fold_in(jax.random.fold_in(key_of[9], part), 71), part),
        "image_keys": draw_image_keys(jax.random.fold_in(jax.random.fold_in(key_of[9], part), 71), part),
        "image_values": noise(part_keys[4], (NIMG * IMG, KVH * HD), 1.0, 6.0, ((0, 16), (1, 4))),
        "cross_lo": draw_cross_lo(jax.random.fold_in(jax.random.fold_in(key_of[9], part), 71), part),
        "cross_hi": draw_cross_hi(jax.random.fold_in(jax.random.fold_in(key_of[9], part), 71), part),
        "query_gain": jnp.clip(jnp.exp(jax.random.uniform(key_of[7], (HD,), jnp.float32, math.log(0.5), math.log(2.0))), 0.5, 2.0),
        "cross_gate": jnp.clip(jax.random.uniform(key_of[8], (H,), jnp.float32, -1.5, 1.5) * levels(key_of[8], (H,), ((0, 4),), -0.4, 0.0), -1.5, 1.5),
    }


NEG = -1e+30
EPS = 1e-05

def attend_rows(query_rows, key_rows, value_rows, allowed):
    scores = jnp.einsum('tgd,sd->gts', query_rows.astype(jnp.float32), key_rows.astype(jnp.float32), precision=lax.Precision.HIGHEST) * (1.0 / math.sqrt(HD))
    scores = jnp.where(allowed[None], scores, NEG)
    highest = lax.optimization_barrier(jnp.max(scores, axis=-1, keepdims=True))
    weights = jnp.where(allowed[None], jnp.exp(scores - highest), 0.0)
    weight_sum = lax.optimization_barrier(jnp.sum(weights, axis=-1))
    combined = jnp.einsum('gts,sd->gtd', weights.astype(jnp.bfloat16).astype(jnp.float32), value_rows.astype(jnp.float32), precision=lax.Precision.HIGHEST)
    return (combined, weight_sum)

def all_heads(query_all, key_all, value_all, allowed_fn, floor_value):
    length = query_all.shape[0]
    tile_rows = math.gcd(length, 512)
    tiles = length // tile_rows
    kv_heads = key_all.shape[1] // HD
    groups = query_all.shape[1] // HD // kv_heads
    query_split = query_all.reshape(length, kv_heads, groups, HD)
    key_split = key_all.reshape(-1, kv_heads, HD)
    value_split = value_all.reshape(-1, kv_heads, HD)

    def one_head(head_index):
        query_head = lax.dynamic_index_in_dim(query_split, head_index, 1, keepdims=False)
        key_head = lax.dynamic_index_in_dim(key_split, head_index, 1, keepdims=False)
        value_head = lax.dynamic_index_in_dim(value_split, head_index, 1, keepdims=False)

        def one_tile(tile_index):
            first_row = tile_index * tile_rows
            query_rows = lax.dynamic_slice_in_dim(query_head, first_row, tile_rows, 0)
            combined, weight_sum = attend_rows(query_rows, key_head, value_head, allowed_fn(first_row, tile_rows))
            return combined / jnp.maximum(weight_sum, floor_value)[..., None]
        return lax.map(one_tile, jnp.arange(tiles, dtype=jnp.int32))
    stacked = lax.map(one_head, jnp.arange(kv_heads, dtype=jnp.int32))
    return stacked.transpose(1, 3, 0, 2, 4).reshape(length, kv_heads * groups * HD)

def reference(queries, keys, values, image_keys, image_values, cross_lo, cross_hi, query_gain, cross_gate):
    length = queries.shape[0]
    positions = jnp.arange(length, dtype=jnp.int32)

    def causal(first_row, tile_rows):
        query_pos = first_row + jnp.arange(tile_rows, dtype=jnp.int32)
        return positions[None, :] <= query_pos[:, None]
    self_heads = all_heads(queries, keys, values, causal, 0.0).astype(jnp.bfloat16)
    heads_wide = self_heads.astype(jnp.float32).reshape(length, -1, HD)
    scaling = lax.rsqrt(lax.optimization_barrier(jnp.mean(heads_wide * heads_wide, axis=-1, keepdims=True)) + EPS)
    cross_queries = (heads_wide * scaling * query_gain).astype(jnp.bfloat16).reshape(length, -1)
    image_index = jnp.arange(image_keys.shape[0], dtype=jnp.int32)

    def ranged(first_row, tile_rows):
        lower = lax.dynamic_slice_in_dim(cross_lo, first_row, tile_rows, 0)
        upper = lax.dynamic_slice_in_dim(cross_hi, first_row, tile_rows, 0)
        return (image_index[None, :] >= lower[:, None]) & (image_index[None, :] < upper[:, None])
    attended = all_heads(cross_queries, image_keys, image_values, ranged, 1.0).reshape(length, -1, HD)
    has_image = (cross_hi > cross_lo)[:, None, None]
    gated = jnp.where(has_image, attended * jnp.tanh(cross_gate)[None, :, None], 0.0)
    return (self_heads, gated.reshape(length, -1).astype(jnp.bfloat16))
```

```python
import math

import jax
import jax.numpy as jnp
from jax import lax
from jax.experimental import pallas as pl
from jax.experimental.pallas import tpu as pltpu
from jax.sharding import PartitionSpec as P

HD = 128
IMG = 2048
EPS = 1e-05
NEG = -1e30
LEVELS = 8
HEADS = 8
LAST = 6
MESH = pl.DeviceIdType.MESH
SCALE = 1.4426950408889634 / math.sqrt(HD)


def dot_nt(a, b):
    return lax.dot_general(a, b, (((1,), (1,)), ((), ())), preferred_element_type=jnp.float32)


def dot_nn(a, b):
    return lax.dot_general(a, b, (((1,), (0,)), ((), ())), preferred_element_type=jnp.float32)


def split_scaled(x):
    x = x * SCALE
    high = x.astype(jnp.bfloat16)
    low = (x - high.astype(jnp.float32)).astype(jnp.bfloat16)
    return high, low


def kernel(
    q_ref, k_ref, v_ref, ik_ref, iv_ref, allow_ref, gain_ref, gate_ref,
    self_ref, cross_ref,
    kv, st_self, st_img, q_in, allow_in, split_q, peak, mixed, allowed,
    st_so, st_co, so_in, co_in, keys2, values1,
    z_send, z_recv, x_send, x_recv,
):
    me = lax.axis_index("ctx")
    z, half = me // 2, me % 2
    rows = q_ref.shape[0]
    img_rows = ik_ref.shape[0]
    wide = HEADS * HD
    partner = {"ctx": z * 2 + (1 - half)}
    up = {"ctx": lax.rem(z + 1, LEVELS) * 2 + half}
    down = {"ctx": lax.rem(z + LEVELS - 1, LEVELS) * 2 + half}

    barrier = pltpu.get_barrier_semaphore()
    for other in (partner, up, down):
        pl.semaphore_signal(barrier, inc=1, device_id=other, device_id_type=MESH)

    own_col = pl.ds(pl.multiple_of(half * HD, HD), HD)
    other_col = pl.ds(pl.multiple_of((1 - half) * HD, HD), HD)
    own_wide = pl.ds(pl.multiple_of(half * wide, wide), wide)
    other_wide = pl.ds(pl.multiple_of((1 - half) * wide, wide), wide)

    def part(kind, level, h):
        if kind == 0:
            start = lax.rem(level, 2) * 2 * rows + h * rows
            return kv.at[level // 2, pl.ds(pl.multiple_of(start, rows), rows), :]
        start = h * img_rows
        return kv.at[LEVELS // 2 + level, pl.ds(pl.multiple_of(start, img_rows), img_rows), :]

    for kind, stage, key_ref, value_ref in (
        (0, st_self, k_ref, v_ref),
        (1, st_img, ik_ref, iv_ref),
    ):
        mine = part(kind, z, half)
        mine[:, :HD] = key_ref[:, own_col]
        mine[:, HD:] = value_ref[:, own_col]
        stage[:, :HD] = key_ref[:, other_col]
        stage[:, HD:] = value_ref[:, other_col]

    def x_copy(slot, src, dst):
        return pltpu.make_async_remote_copy(
            src_ref=src, dst_ref=dst, send_sem=x_send.at[slot], recv_sem=x_recv.at[slot],
            device_id=partner, device_id_type=MESH,
        )

    x_self = x_copy(0, st_self, part(0, z, half))
    x_query = x_copy(1, q_ref.at[:, other_wide], q_in)
    x_allow = x_copy(2, allow_ref, allow_in)
    x_img = x_copy(3, st_img, part(1, z, half))
    x_so = x_copy(4, st_so, so_in)

    def x_co(pair):
        cols = pl.ds(pair * 2 * HD, 2 * HD)
        return x_copy(5 + pair, st_co.at[1, :, cols], co_in.at[:, cols])

    def z_copy(kind, d, n, level, h):
        return pltpu.make_async_remote_copy(
            src_ref=part(kind, level, h), dst_ref=part(kind, level, h),
            send_sem=z_send.at[kind, d, n], recv_sem=z_recv.at[kind, d, n],
            device_id=(up, down)[d], device_id_type=MESH,
        )

    def half_of(d, n):
        if n == LAST:
            return (half, 1 - half)[d]
        return (half, 1 - half)[n % 2]

    def outgoing(kind, d, n):
        level = (z + LEVELS - n // 2, z + n // 2)[d]
        return z_copy(kind, d, n, lax.rem(level, LEVELS), half_of(d, n))

    def incoming(kind, d, n):
        level = (z + LEVELS - 1 - n // 2, z + 1 + n // 2)[d]
        return z_copy(kind, d, n, lax.rem(level, LEVELS), half_of(d, n))

    got = set()

    def await_in(kind, d, n):
        if (kind, d, n) not in got:
            got.add((kind, d, n))
            incoming(kind, d, n).wait_recv()

    def forward(kind, n, ways=(0, 1)):
        for d in ways:
            if n >= 2:
                await_in(kind, d, 5 if (n == LAST and d == 1) else n - 2)
            outgoing(kind, d, n).start()

    def query_rows(slot, h, x):
        high, low = split_scaled(x)
        split_q[slot, h, :, :HD] = high
        split_q[slot, h, :, HD:] = low

    def prepare(slot, read):
        def one(h, _):
            cols = pl.ds(pl.multiple_of(h * HD, HD), HD)
            query_rows(slot, h, read(cols).astype(jnp.float32))
            return 0
        lax.fori_loop(0, HEADS, one, 0)

    def load(piece):
        keys = kv[piece, :, :HD]
        keys2[:, :HD] = keys
        keys2[:, HD:] = keys
        values1[:, :HD] = kv[piece, :, HD:]

    def scores_of(tile, mask=None):
        scores = dot_nt(split_q[tile], keys2[...])
        return scores if mask is None else jnp.where(mask(tile[0], scores.shape), scores, NEG)

    def fold(scores, state, seen=None):
        top = jnp.max(scores, axis=1, keepdims=True)
        if seen is not None:
            top = jnp.where(seen, top, NEG)
        if state is not None:
            top = jnp.maximum(state[0], top)
        shift = top if seen is None else jnp.where(seen, top, -NEG)
        weights = jnp.exp2(scores - shift).astype(jnp.bfloat16)
        term = dot_nn(weights, values1[...])
        if state is not None:
            term = state[1] * jnp.exp2(state[0] - top) + term
        return top, term

    def held(tile):
        return peak[tile][:, :1], mixed[tile]

    def keep(tile, state):
        peak[tile] = jnp.broadcast_to(state[0], peak.shape[2:])
        mixed[tile] = state[1]

    def seen_by(slot, group):
        return allowed[slot, group][:, :1] > 0.5

    def own_order(slot):
        return lax.rem(half + slot, 2)

    def attend(tiles, first=False, mask=None, group=None):
        following = scores_of(tiles[0], mask)
        views = {}
        for n, tile in enumerate(tiles):
            scores = following
            if n + 1 < len(tiles):
                following = scores_of(tiles[n + 1], mask)
            if group is not None and id(tile[0]) not in views:
                views[id(tile[0])] = seen_by(tile[0], group)
            seen = views.get(id(tile[0]))
            keep(tile, fold(scores, None if first else held(tile), seen))

    both = [(s, h) for h in range(HEADS) for s in (0, 1)]

    def causal(slot, shape):
        at_row = z * 2 * rows + own_order(slot) * rows
        at_key = (z // 2) * 4 * rows
        row = at_row - at_key + lax.broadcasted_iota(jnp.int32, shape, 0)
        return lax.broadcasted_iota(jnp.int32, shape, 1) <= row

    values1[:, HD:] = jnp.ones((4 * rows, HD), jnp.bfloat16)

    pl.semaphore_wait(barrier, 3)
    x_self.start()
    forward(0, 0)
    prepare(0, lambda cols: q_ref[:, pl.ds(pl.multiple_of(half * wide + cols.start, HD), HD)])
    x_self.wait_recv()
    x_query.start()
    forward(0, 1)
    forward(0, 2)
    forward(0, 3)

    early = jnp.where(lax.rem(z, 2) == 1, 0, 2)

    def begin(slot, _):
        @pl.when(slot == 1)
        def _():
            x_query.wait_recv()
            x_allow.start()
            x_img.start()
            prepare(1, lambda cols: q_in[:, cols])

        tiles = [(slot, h) for h in range(HEADS)]
        load(z // 2)
        attend(tiles, True, causal)

        @pl.when(slot == 0)
        def _():
            forward(0, 4)
            forward(0, 5)

        @pl.when(z >= 6)
        def _():
            load(early)
            attend(tiles)

        @pl.when(slot == 0)
        def _():
            forward(0, 6)
            forward(1, 0)
        return 0

    lax.fori_loop(0, 2, begin, 0)
    x_img.wait_recv()
    forward(1, 1)
    for d in (0, 1):
        for n in (4, 5, 6):
            await_in(0, d, n)
    x_allow.wait_recv()
    for slot, ref in ((0, allow_ref), (1, allow_in)):
        for image in range(4):
            allowed[slot, image] = jnp.broadcast_to(
                ref[:, image:image + 1].astype(jnp.float32), allowed.shape[2:]
            )
        allowed[slot, 4] = jnp.ones(allowed.shape[2:], jnp.float32)

    def finish_self(h, _):
        cols = pl.ds(pl.multiple_of(h * HD, HD), HD)
        for slot in (1, 0):
            acc = mixed[slot, h]
            out = (acc[:, :HD] / acc[:, HD:]).astype(jnp.bfloat16)
            if slot == 0:
                self_ref[:, pl.ds(pl.multiple_of(half * wide + h * HD, HD), HD)] = out
            else:
                st_so[:, cols] = out
            x = out.astype(jnp.float32)
            norm = lax.rsqrt(jnp.mean(x * x, axis=1, keepdims=True) + EPS)
            x = (x * norm).reshape(rows // 8, 8, HD) * gain_ref[...][None]
            x = x.reshape(rows, HD).astype(jnp.bfloat16)
            query_rows(slot, h, x.astype(jnp.float32))
            peak[slot, h] = jnp.full(peak.shape[2:], NEG, jnp.float32)
            mixed[slot, h] = jnp.zeros(mixed.shape[2:], jnp.float32)
        return 0

    def image_level(step):
        away = jnp.where(lax.rem(step, 2) == 0, step // 2, LEVELS - (step + 1) // 2)
        return lax.rem(z + away, LEVELS)

    def advance(step, _):
        @pl.when(step == 1)
        def _():
            forward(1, 2)

        @pl.when(step == 2)
        def _():
            forward(1, 3)
            lax.fori_loop(0, HEADS, finish_self, 0)
            x_so.start()

        @pl.when(step == 3)
        def _():
            forward(1, 4)

        @pl.when(step == 4)
        def _():
            forward(1, 5)

        @pl.when(step == 5)
        def _():
            forward(1, 6, (0,))

        @pl.when(step == 6)
        def _():
            forward(1, 6, (1,))

        level = image_level(jnp.maximum(step - 2, 0))
        text = jnp.where(step == 1, 1, jnp.where(z >= 6, 2 - early, 0))
        piece = jnp.where(step < 2, text, LEVELS // 2 + level)
        group = jnp.where(step < 2, 4, level // 2)

        @pl.when((step >= 2) | (z >= 2 + 2 * step))
        def _():
            load(piece)
            attend(both, group=group)
        return 0

    lax.fori_loop(0, 7, advance, 0)
    for d in (0, 1):
        await_in(1, d, 4)
        await_in(1, d, 5)

    def finish(turn, _):
        slot = 1 - turn
        tiles = [(slot, h) for h in range(HEADS)]

        def more(step, _):
            level = image_level(step)
            load(LEVELS // 2 + level)
            attend(tiles, group=level // 2)
            return 0

        lax.fori_loop(5, 7, more, 0)

        @pl.when(slot == 1)
        def _():
            x_so.wait_recv()
            self_ref[:, other_wide] = so_in[...]
            for d in (0, 1):
                await_in(1, d, 6)

        level = image_level(7)
        load(LEVELS // 2 + level)
        seen = seen_by(slot, level // 2)
        following = scores_of(tiles[0])
        for h, tile in enumerate(tiles):
            scores = following
            if h + 1 < HEADS:
                following = scores_of(tiles[h + 1])
            _, acc = fold(scores, held(tile), seen)
            gate = jnp.tanh(gate_ref[half * HEADS + h])[None]
            out = (acc[:, :HD] / jnp.maximum(acc[:, HD:], 1.0)).reshape(rows // 8, 8, HD) * gate
            st_co[slot, :, h * HD:(h + 1) * HD] = out.reshape(rows, HD).astype(jnp.bfloat16)
            if h % 2 == 1:
                @pl.when(slot == 1)
                def _():
                    x_co(h // 2).start()
        return 0

    lax.fori_loop(0, 2, finish, 0)
    cross_ref[:, own_wide] = st_co[0]
    for pair in range(HEADS // 2):
        x_co(pair).wait_recv()
    cross_ref[:, other_wide] = co_in[...]

    for copy in (x_self, x_query, x_allow, x_img, x_so):
        copy.wait_send()
    for pair in range(HEADS // 2):
        x_co(pair).wait_send()
    for kind in (0, 1):
        for d in (0, 1):
            for n in range(LAST + 1):
                outgoing(kind, d, n).wait_send()


def per_device(
    queries, keys, values, image_keys, image_values, cross_lo, cross_hi, query_gain, cross_gate
):
    rows, img_rows = queries.shape[0], image_keys.shape[0]
    wide = HEADS * HD
    first = jnp.arange(HD, dtype=jnp.int32)[None, :] * IMG
    allow = ((cross_lo[:, None] <= first) & (first < cross_hi[:, None])).astype(jnp.bfloat16)
    gate = jnp.broadcast_to(cross_gate[:, None, None], (cross_gate.shape[0], 8, HD))
    vmem = pl.BlockSpec(memory_space=pltpu.VMEM)
    bf16, f32 = jnp.bfloat16, jnp.float32
    return pl.pallas_call(
        kernel,
        out_shape=(jax.ShapeDtypeStruct(queries.shape, bf16),) * 2,
        in_specs=[vmem] * 8,
        out_specs=(vmem, vmem),
        scratch_shapes=[
            pltpu.VMEM((LEVELS // 2 + LEVELS, 4 * rows, 2 * HD), bf16),
            pltpu.VMEM((rows, 2 * HD), bf16),
            pltpu.VMEM((img_rows, 2 * HD), bf16),
            pltpu.VMEM((rows, wide), bf16),
            pltpu.VMEM((rows, HD), bf16),
            pltpu.VMEM((2, HEADS, rows, 2 * HD), bf16),
            pltpu.VMEM((2, HEADS, rows, HD), f32),
            pltpu.VMEM((2, HEADS, rows, 2 * HD), f32),
            pltpu.VMEM((2, 5, rows, HD), f32),
            pltpu.VMEM((rows, wide), bf16),
            pltpu.VMEM((2, rows, wide), bf16),
            pltpu.VMEM((rows, wide), bf16),
            pltpu.VMEM((rows, wide), bf16),
            pltpu.VMEM((4 * rows, 2 * HD), bf16),
            pltpu.VMEM((4 * rows, 2 * HD), bf16),
            pltpu.SemaphoreType.DMA((2, 2, LAST + 1)),
            pltpu.SemaphoreType.DMA((2, 2, LAST + 1)),
            pltpu.SemaphoreType.DMA((9,)),
            pltpu.SemaphoreType.DMA((9,)),
        ],
        compiler_params=pltpu.CompilerParams(
            collective_id=0, has_side_effects=True, vmem_limit_bytes=56 * 2**20
        ),
    )(queries, keys, values, image_keys, image_values, allow, jnp.broadcast_to(query_gain, (8, HD)), gate)


def solution(mesh):
    split = P(("doc", "ctx"), "head")
    return jax.shard_map(
        per_device,
        mesh=mesh,
        in_specs=(split,) * 5 + (P(("doc", "ctx")), P(("doc", "ctx")), P(), P("head")),
        out_specs=(split, split),
        check_vma=False,
    )
```

```python
import math

import jax
import jax.numpy as jnp
from jax import lax
from jax.experimental import pallas as pl
from jax.experimental.pallas import tpu as pltpu
from jax.sharding import PartitionSpec as P

HD = 128
IMG = 2048
EPS = 1e-05
NEG = -1e30
LEVELS = 8
HEADS = 8
LAST = 6
MESH = pl.DeviceIdType.MESH
SCALE = 1.4426950408889634 / math.sqrt(HD)


def dot_nt(a, b):
    return lax.dot_general(a, b, (((1,), (1,)), ((), ())), preferred_element_type=jnp.float32)


def dot_nn(a, b):
    return lax.dot_general(a, b, (((1,), (0,)), ((), ())), preferred_element_type=jnp.float32)


def split_scaled(x):
    x = x * SCALE
    high = x.astype(jnp.bfloat16)
    low = (x - high.astype(jnp.float32)).astype(jnp.bfloat16)
    return high, low


def kernel(
    q_hbm, k_hbm, v_hbm, ik_hbm, iv_hbm, low_hbm, high_hbm, gain_hbm, gate_hbm,
    self_ref, cross_ref,
    kv, st_self, st_img, q_in, allow_in, split_q, peak, mixed, allowed,
    st_so, st_co, so_in, co_in, keys2, values1, allow_ref,
    q_own, q_out, low_ref, high_ref, gain_ref, gate_ref,
    load_sem, z_send, z_recv, x_send, x_recv,
):
    me = lax.axis_index("ctx")
    z, half = me // 2, me % 2
    rows = q_hbm.shape[0]
    img_rows = ik_hbm.shape[0]
    wide = HEADS * HD
    partner = {"ctx": z * 2 + (1 - half)}
    up = {"ctx": lax.rem(z + 1, LEVELS) * 2 + half}
    down = {"ctx": lax.rem(z + LEVELS - 1, LEVELS) * 2 + half}

    barrier = pltpu.get_barrier_semaphore()
    for other in (partner, up, down):
        pl.semaphore_signal(barrier, inc=1, device_id=other, device_id_type=MESH)

    own_col = pl.ds(pl.multiple_of(half * HD, HD), HD)
    other_col = pl.ds(pl.multiple_of((1 - half) * HD, HD), HD)
    own_wide = pl.ds(pl.multiple_of(half * wide, wide), wide)
    other_wide = pl.ds(pl.multiple_of((1 - half) * wide, wide), wide)

    def part(kind, level, h):
        if kind == 0:
            start = lax.rem(level, 2) * 2 * rows + h * rows
            return kv.at[level // 2, pl.ds(pl.multiple_of(start, rows), rows), :]
        start = h * img_rows
        return kv.at[LEVELS // 2 + level, pl.ds(pl.multiple_of(start, img_rows), img_rows), :]

    fetches = []

    def fetch(src, dst):
        copy = pltpu.make_async_copy(src, dst, load_sem.at[len(fetches)])
        fetches.append(copy)
        copy.start()

    for kind, stage, key_hbm, value_hbm in (
        (0, st_self, k_hbm, v_hbm),
        (1, st_img, ik_hbm, iv_hbm),
    ):
        mine = part(kind, z, half)
        fetch(key_hbm.at[:, own_col], mine.at[:, pl.ds(0, HD)])
        fetch(value_hbm.at[:, own_col], mine.at[:, pl.ds(HD, HD)])
        fetch(key_hbm.at[:, other_col], stage.at[:, pl.ds(0, HD)])
        fetch(value_hbm.at[:, other_col], stage.at[:, pl.ds(HD, HD)])
        if kind == 0:
            fetch(q_hbm.at[:, own_wide], q_own)
            fetch(q_hbm.at[:, other_wide], q_out)
    for src, dst in ((low_hbm, low_ref), (high_hbm, high_ref), (gain_hbm, gain_ref), (gate_hbm, gate_ref)):
        fetch(src, dst)

    def x_copy(slot, src, dst):
        return pltpu.make_async_remote_copy(
            src_ref=src, dst_ref=dst, send_sem=x_send.at[slot], recv_sem=x_recv.at[slot],
            device_id=partner, device_id_type=MESH,
        )

    x_self = x_copy(0, st_self, part(0, z, half))
    x_query = x_copy(1, q_out, q_in)
    x_allow = x_copy(2, allow_ref, allow_in)
    x_img = x_copy(3, st_img, part(1, z, half))
    x_so = x_copy(4, st_so, so_in)

    def x_co(pair):
        cols = pl.ds(pair * 2 * HD, 2 * HD)
        return x_copy(5 + pair, st_co.at[1, :, cols], co_in.at[:, cols])

    def z_copy(kind, d, n, level, h):
        return pltpu.make_async_remote_copy(
            src_ref=part(kind, level, h), dst_ref=part(kind, level, h),
            send_sem=z_send.at[kind, d, n], recv_sem=z_recv.at[kind, d, n],
            device_id=(up, down)[d], device_id_type=MESH,
        )

    def half_of(d, n):
        if n == LAST:
            return (half, 1 - half)[d]
        return (half, 1 - half)[n % 2]

    def outgoing(kind, d, n):
        level = (z + LEVELS - n // 2, z + n // 2)[d]
        return z_copy(kind, d, n, lax.rem(level, LEVELS), half_of(d, n))

    def incoming(kind, d, n):
        level = (z + LEVELS - 1 - n // 2, z + 1 + n // 2)[d]
        return z_copy(kind, d, n, lax.rem(level, LEVELS), half_of(d, n))

    got = set()

    def await_in(kind, d, n):
        if (kind, d, n) not in got:
            got.add((kind, d, n))
            incoming(kind, d, n).wait_recv()

    def forward(kind, n, ways=(0, 1)):
        for d in ways:
            if n >= 2:
                await_in(kind, d, 5 if (n == LAST and d == 1) else n - 2)
            outgoing(kind, d, n).start()

    def query_rows(slot, h, x):
        high, low = split_scaled(x)
        split_q[slot, h, :, :HD] = high
        split_q[slot, h, :, HD:] = low

    def prepare(slot, read):
        def one(h, _):
            cols = pl.ds(pl.multiple_of(h * HD, HD), HD)
            query_rows(slot, h, read(cols).astype(jnp.float32))
            return 0
        lax.fori_loop(0, HEADS, one, 0)

    def load(piece):
        keys = kv[piece, :, :HD]
        keys2[:, :HD] = keys
        keys2[:, HD:] = keys
        values1[:, :HD] = kv[piece, :, HD:]

    def scores_of(tile, mask=None):
        scores = dot_nt(split_q[tile], keys2[...])
        return scores if mask is None else jnp.where(mask(tile[0], scores.shape), scores, NEG)

    def fold(scores, state, seen=None):
        top = jnp.max(scores, axis=1, keepdims=True)
        if seen is not None:
            top = jnp.where(seen, top, NEG)
        if state is not None:
            top = jnp.maximum(state[0], top)
        shift = top if seen is None else jnp.where(seen, top, -NEG)
        weights = jnp.exp2(scores - shift).astype(jnp.bfloat16)
        term = dot_nn(weights, values1[...])
        if state is not None:
            term = state[1] * jnp.exp2(state[0] - top) + term
        return top, term

    def held(tile):
        return peak[tile][:, :1], mixed[tile]

    def keep(tile, state):
        peak[tile] = jnp.broadcast_to(state[0], peak.shape[2:])
        mixed[tile] = state[1]

    def seen_by(slot, group):
        return allowed[slot, group][:, :1] > 0.5

    def own_order(slot):
        return lax.rem(half + slot, 2)

    def attend(tiles, first=False, mask=None, group=None):
        following = scores_of(tiles[0], mask)
        views = {}
        for n, tile in enumerate(tiles):
            scores = following
            if n + 1 < len(tiles):
                following = scores_of(tiles[n + 1], mask)
            if group is not None and id(tile[0]) not in views:
                views[id(tile[0])] = seen_by(tile[0], group)
            seen = views.get(id(tile[0]))
            keep(tile, fold(scores, None if first else held(tile), seen))

    both = [(s, h) for h in range(HEADS) for s in (0, 1)]

    def causal(slot, shape):
        at_row = z * 2 * rows + own_order(slot) * rows
        at_key = (z // 2) * 4 * rows
        row = at_row - at_key + lax.broadcasted_iota(jnp.int32, shape, 0)
        return lax.broadcasted_iota(jnp.int32, shape, 1) <= row

    values1[:, HD:] = jnp.ones((4 * rows, HD), jnp.bfloat16)

    for copy in fetches[:4]:
        copy.wait()
    pl.semaphore_wait(barrier, 3)
    x_self.start()
    forward(0, 0)
    for copy in fetches[4:]:
        copy.wait()
    prepare(0, lambda cols: q_own[:, cols])
    x_self.wait_recv()
    x_query.start()
    forward(0, 1)
    lane = lax.broadcasted_iota(jnp.int32, (HD, HD), 1)
    diagonal = lane == lax.broadcasted_iota(jnp.int32, (HD, HD), 0)

    def column(ref, block):
        wide_row = jnp.broadcast_to(ref[block:block + 1, :].astype(jnp.float32), (HD, HD))
        return jnp.sum(jnp.where(diagonal, wide_row, 0.0), axis=1, keepdims=True)

    begins = (lane * IMG).astype(jnp.float32)
    for block in range(rows // HD):
        inside = (column(low_ref, block) <= begins) & (begins < column(high_ref, block))
        allow_ref[block * HD:(block + 1) * HD, :] = jnp.where(inside, 1.0, 0.0).astype(jnp.bfloat16)
    forward(0, 2)
    forward(0, 3)

    early = jnp.where(lax.rem(z, 2) == 1, 0, 2)

    def begin(slot, _):
        @pl.when(slot == 1)
        def _():
            x_query.wait_recv()
            x_allow.start()
            x_img.start()
            prepare(1, lambda cols: q_in[:, cols])

        tiles = [(slot, h) for h in range(HEADS)]
        load(z // 2)
        attend(tiles, True, causal)

        @pl.when(slot == 0)
        def _():
            forward(0, 4)
            forward(0, 5)

        def more(step, _):
            @pl.when((slot == 0) & (step == 1))
            def _():
                forward(0, 6)
                forward(1, 0)
                for d in (0, 1):
                    await_in(0, d, 4)
                    await_in(0, d, 5)

            @pl.when((slot == 1) & (step == 1))
            def _():
                x_img.wait_recv()
                forward(1, 1)

            @pl.when(z >= 6)
            def _():
                load(jnp.where(step == 0, early, 2 - early))
                attend(tiles)
            return 0

        lax.fori_loop(0, 2, more, 0)
        return 0

    lax.fori_loop(0, 2, begin, 0)
    for d in (0, 1):
        await_in(0, d, 6)
    x_allow.wait_recv()
    for slot, ref in ((0, allow_ref), (1, allow_in)):
        for image in range(4):
            allowed[slot, image] = jnp.broadcast_to(
                ref[:, image:image + 1].astype(jnp.float32), allowed.shape[2:]
            )
        allowed[slot, 4] = jnp.ones(allowed.shape[2:], jnp.float32)

    def finish_self(pair, _):
        for slot, h in ((s, pair * 2 + u) for u in (0, 1) for s in (1, 0)):
            cols = pl.ds(pl.multiple_of(h * HD, HD), HD)
            acc = mixed[slot, h]
            out = (acc[:, :HD] / acc[:, HD:]).astype(jnp.bfloat16)
            if slot == 0:
                self_ref[:, pl.ds(pl.multiple_of(half * wide + h * HD, HD), HD)] = out
            else:
                st_so[:, cols] = out
            x = out.astype(jnp.float32)
            norm = lax.rsqrt(jnp.mean(x * x, axis=1, keepdims=True) + EPS)
            x = (x * norm * gain_ref[...]).astype(jnp.bfloat16)
            query_rows(slot, h, x.astype(jnp.float32))
            peak[slot, h] = jnp.full(peak.shape[2:], NEG, jnp.float32)
            mixed[slot, h] = jnp.zeros(mixed.shape[2:], jnp.float32)
        return 0

    def image_level(step):
        away = jnp.where(lax.rem(step, 2) == 0, step // 2, LEVELS - (step + 1) // 2)
        return lax.rem(z + away, LEVELS)

    def advance(step, _):
        @pl.when(step == 2)
        def _():
            forward(1, 2)
            lax.fori_loop(0, HEADS // 2, finish_self, 0)
            x_so.start()
            forward(1, 3)

        @pl.when(step == 3)
        def _():
            forward(1, 4)

        @pl.when(step == 4)
        def _():
            forward(1, 5)

        @pl.when(step == 5)
        def _():
            forward(1, 6, (0,))

        @pl.when(step == 6)
        def _():
            forward(1, 6, (1,))

        level = image_level(jnp.maximum(step - 2, 0))
        text = jnp.where(step == 1, 1, 0)
        piece = jnp.where(step < 2, text, LEVELS // 2 + level)
        group = jnp.where(step < 2, 4, level // 2)

        @pl.when((step >= 2) | ((z >= 2 + 2 * step) & ((step == 1) | (z < 6))))
        def _():
            load(piece)
            attend(both, group=group)
        return 0

    lax.fori_loop(0, 7, advance, 0)
    for d in (0, 1):
        await_in(1, d, 4)
        await_in(1, d, 5)

    gate_lane = lax.broadcasted_iota(jnp.int32, gate_ref.shape, 1)

    def finish(turn, _):
        slot = 1 - turn
        tiles = [(slot, h) for h in range(HEADS)]

        def more(step, _):
            level = image_level(step)
            load(LEVELS // 2 + level)
            attend(tiles, group=level // 2)
            return 0

        lax.fori_loop(5, 7, more, 0)

        @pl.when(slot == 1)
        def _():
            x_so.wait_recv()
            self_ref[:, other_wide] = so_in[...]
            for d in (0, 1):
                await_in(1, d, 6)

        level = image_level(7)
        load(LEVELS // 2 + level)
        seen = seen_by(slot, level // 2)
        following = scores_of(tiles[0])
        for h, tile in enumerate(tiles):
            scores = following
            if h + 1 < HEADS:
                following = scores_of(tiles[h + 1])
            _, acc = fold(scores, held(tile), seen)
            gate = jnp.tanh(jnp.sum(
                jnp.where(gate_lane == half * HEADS + h, gate_ref[...], 0.0), axis=1, keepdims=True
            ))
            out = acc[:, :HD] / jnp.maximum(acc[:, HD:], 1.0) * gate
            st_co[slot, :, h * HD:(h + 1) * HD] = out.astype(jnp.bfloat16)
            if h % 2 == 1:
                @pl.when(slot == 1)
                def _():
                    x_co(h // 2).start()
        return 0

    lax.fori_loop(0, 2, finish, 0)
    cross_ref[:, own_wide] = st_co[0]
    for pair in range(HEADS // 2):
        x_co(pair).wait_recv()
    cross_ref[:, other_wide] = co_in[...]

    for copy in (x_self, x_query, x_allow, x_img, x_so):
        copy.wait_send()
    for pair in range(HEADS // 2):
        x_co(pair).wait_send()
    for kind in (0, 1):
        for d in (0, 1):
            for n in range(LAST + 1):
                outgoing(kind, d, n).wait_send()


def per_device(
    queries, keys, values, image_keys, image_values, cross_lo, cross_hi, query_gain, cross_gate
):
    rows, img_rows = queries.shape[0], image_keys.shape[0]
    wide = HEADS * HD
    vmem = pl.BlockSpec(memory_space=pltpu.VMEM)
    bf16, f32 = jnp.bfloat16, jnp.float32
    pin = lambda x: pltpu.with_memory_space_constraint(x, pltpu.HBM)
    return pl.pallas_call(
        kernel,
        out_shape=(jax.ShapeDtypeStruct(queries.shape, bf16),) * 2,
        in_specs=[pl.BlockSpec(memory_space=pltpu.HBM)] * 9,
        out_specs=(vmem, vmem),
        scratch_shapes=[
            pltpu.VMEM((LEVELS // 2 + LEVELS, 4 * rows, 2 * HD), bf16),
            pltpu.VMEM((rows, 2 * HD), bf16),
            pltpu.VMEM((img_rows, 2 * HD), bf16),
            pltpu.VMEM((rows, wide), bf16),
            pltpu.VMEM((rows, HD), bf16),
            pltpu.VMEM((2, HEADS, rows, 2 * HD), bf16),
            pltpu.VMEM((2, HEADS, rows, HD), f32),
            pltpu.VMEM((2, HEADS, rows, 2 * HD), f32),
            pltpu.VMEM((2, 5, rows, HD), f32),
            pltpu.VMEM((rows, wide), bf16),
            pltpu.VMEM((2, rows, wide), bf16),
            pltpu.VMEM((rows, wide), bf16),
            pltpu.VMEM((rows, wide), bf16),
            pltpu.VMEM((4 * rows, 2 * HD), bf16),
            pltpu.VMEM((4 * rows, 2 * HD), bf16),
            pltpu.VMEM((rows, HD), bf16),
            pltpu.VMEM((rows, wide), bf16),
            pltpu.VMEM((rows, wide), bf16),
            pltpu.VMEM((rows // HD, HD), jnp.int32),
            pltpu.VMEM((rows // HD, HD), jnp.int32),
            pltpu.VMEM((1, HD), f32),
            pltpu.VMEM((1, cross_gate.shape[0]), f32),
            pltpu.SemaphoreType.DMA((14,)),
            pltpu.SemaphoreType.DMA((2, 2, LAST + 1)),
            pltpu.SemaphoreType.DMA((2, 2, LAST + 1)),
            pltpu.SemaphoreType.DMA((9,)),
            pltpu.SemaphoreType.DMA((9,)),
        ],
        compiler_params=pltpu.CompilerParams(
            collective_id=0, has_side_effects=True, vmem_limit_bytes=40 * 2**20
        ),
    )(
        *(pin(x) for x in (queries, keys, values, image_keys, image_values)),
        pin(cross_lo.reshape(-1, HD)), pin(cross_hi.reshape(-1, HD)), pin(query_gain[None, :]),
        pin(cross_gate[None, :]),
    )


def solution(mesh):
    split = P(("doc", "ctx"), "head")
    return jax.shard_map(
        per_device,
        mesh=mesh,
        in_specs=(split,) * 5 + (P(("doc", "ctx")), P(("doc", "ctx")), P(), P("head")),
        out_specs=(split, split),
        check_vma=False,
    )
```

```python
import math

import jax
import jax.numpy as jnp
from jax import lax
from jax.experimental import pallas as pl
from jax.experimental.pallas import tpu as pltpu
from jax.sharding import PartitionSpec as P

HD = 128
IMG = 2048
EPS = 1e-05
NEG = -1e30
LEVELS = 8
HEADS = 8
LAST = 6
MESH = pl.DeviceIdType.MESH
SCALE = 1.4426950408889634 / math.sqrt(HD)


def dot_nt(a, b):
    return lax.dot_general(a, b, (((1,), (1,)), ((), ())), preferred_element_type=jnp.float32)


def dot_nn(a, b):
    return lax.dot_general(a, b, (((1,), (0,)), ((), ())), preferred_element_type=jnp.float32)


def split_scaled(x):
    x = x * SCALE
    high = x.astype(jnp.bfloat16)
    low = (x - high.astype(jnp.float32)).astype(jnp.bfloat16)
    return high, low


def kernel(
    q_hbm, k_hbm, v_hbm, ik_hbm, iv_hbm, low_hbm, high_hbm, gain_hbm, gate_hbm,
    self_ref, cross_ref,
    kv, st_self, st_img, q_in, allow_in, split_q, peak, mixed, allowed,
    st_so, st_co, so_in, co_in, keys2, values1, allow_ref,
    q_own, q_out, low_ref, high_ref, gain_ref, gate_ref,
    load_sem, z_send, z_recv, x_send, x_recv,
):
    me = lax.axis_index("ctx")
    z, half = me // 2, me % 2
    rows = q_hbm.shape[0]
    img_rows = ik_hbm.shape[0]
    wide = HEADS * HD
    partner = {"ctx": z * 2 + (1 - half)}
    up = {"ctx": lax.rem(z + 1, LEVELS) * 2 + half}
    down = {"ctx": lax.rem(z + LEVELS - 1, LEVELS) * 2 + half}

    barrier = pltpu.get_barrier_semaphore()
    for other in (partner, up, down):
        pl.semaphore_signal(barrier, inc=1, device_id=other, device_id_type=MESH)

    own_col = pl.ds(pl.multiple_of(half * HD, HD), HD)
    other_col = pl.ds(pl.multiple_of((1 - half) * HD, HD), HD)
    own_wide = pl.ds(pl.multiple_of(half * wide, wide), wide)
    other_wide = pl.ds(pl.multiple_of((1 - half) * wide, wide), wide)

    def part(kind, level, h):
        if kind == 0:
            start = lax.rem(level, 2) * 2 * rows + h * rows
            return kv.at[level // 2, pl.ds(pl.multiple_of(start, rows), rows), :]
        start = h * img_rows
        return kv.at[LEVELS // 2 + level, pl.ds(pl.multiple_of(start, img_rows), img_rows), :]

    fetches = []

    def fetch(src, dst):
        copy = pltpu.make_async_copy(src, dst, load_sem.at[len(fetches)])
        fetches.append(copy)
        copy.start()

    for kind, stage, key_hbm, value_hbm in (
        (0, st_self, k_hbm, v_hbm),
        (1, st_img, ik_hbm, iv_hbm),
    ):
        mine = part(kind, z, half)
        fetch(key_hbm.at[:, own_col], mine.at[:, pl.ds(0, HD)])
        fetch(value_hbm.at[:, own_col], mine.at[:, pl.ds(HD, HD)])
        fetch(key_hbm.at[:, other_col], stage.at[:, pl.ds(0, HD)])
        fetch(value_hbm.at[:, other_col], stage.at[:, pl.ds(HD, HD)])
        if kind == 0:
            fetch(q_hbm.at[:, own_wide], q_own)
            fetch(q_hbm.at[:, other_wide], q_out)
    for src, dst in ((low_hbm, low_ref), (high_hbm, high_ref), (gain_hbm, gain_ref), (gate_hbm, gate_ref)):
        fetch(src, dst)

    def x_copy(slot, src, dst):
        return pltpu.make_async_remote_copy(
            src_ref=src, dst_ref=dst, send_sem=x_send.at[slot], recv_sem=x_recv.at[slot],
            device_id=partner, device_id_type=MESH,
        )

    x_self = x_copy(0, st_self, part(0, z, half))
    x_query = x_copy(1, q_out, q_in)
    x_allow = x_copy(2, allow_ref, allow_in)
    x_img = x_copy(3, st_img, part(1, z, half))
    x_so = x_copy(4, st_so, so_in)

    def x_co(pair):
        cols = pl.ds(pair * 2 * HD, 2 * HD)
        return x_copy(5 + pair, st_co.at[1, :, cols], co_in.at[:, cols])

    def z_copy(kind, d, n, level, h):
        return pltpu.make_async_remote_copy(
            src_ref=part(kind, level, h), dst_ref=part(kind, level, h),
            send_sem=z_send.at[kind, d, n], recv_sem=z_recv.at[kind, d, n],
            device_id=(up, down)[d], device_id_type=MESH,
        )

    def half_of(d, n):
        if n == LAST:
            return (half, 1 - half)[d]
        return (half, 1 - half)[n % 2]

    def outgoing(kind, d, n):
        level = (z + LEVELS - n // 2, z + n // 2)[d]
        return z_copy(kind, d, n, lax.rem(level, LEVELS), half_of(d, n))

    def incoming(kind, d, n):
        level = (z + LEVELS - 1 - n // 2, z + 1 + n // 2)[d]
        return z_copy(kind, d, n, lax.rem(level, LEVELS), half_of(d, n))

    got = set()

    def await_in(kind, d, n):
        if (kind, d, n) not in got:
            got.add((kind, d, n))
            incoming(kind, d, n).wait_recv()

    def forward(kind, n, ways=(0, 1)):
        for d in ways:
            if n >= 2:
                await_in(kind, d, 5 if (n == LAST and d == 1) else n - 2)
            outgoing(kind, d, n).start()

    def query_rows(slot, h, x):
        high, low = split_scaled(x)
        split_q[slot, h, :, :HD] = high
        split_q[slot, h, :, HD:] = low

    def prepare(slot, read):
        def one(h, _):
            cols = pl.ds(pl.multiple_of(h * HD, HD), HD)
            query_rows(slot, h, read(cols).astype(jnp.float32))
            return 0
        lax.fori_loop(0, HEADS, one, 0)

    def load(piece):
        keys = kv[piece, :, :HD]
        keys2[:, :HD] = keys
        keys2[:, HD:] = keys
        values1[:, :HD] = kv[piece, :, HD:]

    def scores_of(tile, mask=None):
        scores = dot_nt(split_q[tile], keys2[...])
        return scores if mask is None else jnp.where(mask(tile[0], scores.shape), scores, NEG)

    def fold(scores, state, seen=None):
        top = jnp.max(scores, axis=1, keepdims=True)
        if seen is not None:
            top = jnp.where(seen, top, NEG)
        if state is not None:
            top = jnp.maximum(state[0], top)
        shift = top if seen is None else jnp.where(seen, top, -NEG)
        weights = jnp.exp2(scores - shift).astype(jnp.bfloat16)
        term = dot_nn(weights, values1[...])
        if state is not None:
            term = state[1] * jnp.exp2(state[0] - top) + term
        return top, term

    def held(tile):
        return peak[tile][:, :1], mixed[tile]

    def keep(tile, state):
        peak[tile] = jnp.broadcast_to(state[0], peak.shape[2:])
        mixed[tile] = state[1]

    def seen_by(slot, group):
        return allowed[slot, group][:, :1] > 0.5

    def own_order(slot):
        return lax.rem(half + slot, 2)

    def attend(tiles, first=False, mask=None, group=None, before=lambda tile: None):
        before(tiles[0])
        following = scores_of(tiles[0], mask)
        views = {}
        for n, tile in enumerate(tiles):
            scores = following
            if n + 1 < len(tiles):
                before(tiles[n + 1])
                following = scores_of(tiles[n + 1], mask)
            if group is not None and id(tile[0]) not in views:
                views[id(tile[0])] = seen_by(tile[0], group)
            seen = views.get(id(tile[0]))
            keep(tile, fold(scores, None if first else held(tile), seen))

    both = [(s, h) for h in range(HEADS) for s in (0, 1)]

    def causal(slot, shape):
        at_row = z * 2 * rows + own_order(slot) * rows
        at_key = (z // 2) * 4 * rows
        row = at_row - at_key + lax.broadcasted_iota(jnp.int32, shape, 0)
        return lax.broadcasted_iota(jnp.int32, shape, 1) <= row

    values1[:, HD:] = jnp.ones((4 * rows, HD), jnp.bfloat16)

    for copy in fetches[:4]:
        copy.wait()
    pl.semaphore_wait(barrier, 3)
    x_self.start()
    forward(0, 0)
    for copy in fetches[4:]:
        copy.wait()
    prepare(0, lambda cols: q_own[:, cols])
    x_self.wait_recv()
    x_query.start()
    forward(0, 1)
    lane = lax.broadcasted_iota(jnp.int32, (HD, HD), 1)
    diagonal = lane == lax.broadcasted_iota(jnp.int32, (HD, HD), 0)

    def column(ref, block):
        wide_row = jnp.broadcast_to(ref[block:block + 1, :].astype(jnp.float32), (HD, HD))
        return jnp.sum(jnp.where(diagonal, wide_row, 0.0), axis=1, keepdims=True)

    begins = (lane * IMG).astype(jnp.float32)
    for block in range(rows // HD):
        inside = (column(low_ref, block) <= begins) & (begins < column(high_ref, block))
        allow_ref[block * HD:(block + 1) * HD, :] = jnp.where(inside, 1.0, 0.0).astype(jnp.bfloat16)
    forward(0, 2)
    forward(0, 3)

    early = jnp.where(lax.rem(z, 2) == 1, 0, 2)

    def begin(slot, _):
        @pl.when(slot == 1)
        def _():
            x_query.wait_recv()
            x_allow.start()
            x_img.start()
            prepare(1, lambda cols: q_in[:, cols])

        tiles = [(slot, h) for h in range(HEADS)]
        load(z // 2)
        attend(tiles, True, causal)

        @pl.when(slot == 0)
        def _():
            forward(0, 4)
            forward(0, 5)

        def more(step, _):
            @pl.when((slot == 0) & (step == 1))
            def _():
                forward(0, 6)
                forward(1, 0)
                for d in (0, 1):
                    await_in(0, d, 4)
                    await_in(0, d, 5)

            @pl.when((slot == 1) & (step == 1))
            def _():
                x_img.wait_recv()
                forward(1, 1)

            @pl.when(z >= 6)
            def _():
                load(jnp.where(step == 0, early, 2 - early))
                attend(tiles)
            return 0

        lax.fori_loop(0, 2, more, 0)
        return 0

    lax.fori_loop(0, 2, begin, 0)
    for d in (0, 1):
        await_in(0, d, 6)
    x_allow.wait_recv()
    for slot, ref in ((0, allow_ref), (1, allow_in)):
        for image in range(4):
            allowed[slot, image] = jnp.broadcast_to(
                ref[:, image:image + 1].astype(jnp.float32), allowed.shape[2:]
            )
        allowed[slot, 4] = jnp.ones(allowed.shape[2:], jnp.float32)

    def finish_self(tile):
        slot, h = tile
        acc = mixed[tile]
        out = (acc[:, :HD] / acc[:, HD:]).astype(jnp.bfloat16)
        if slot == 0:
            self_ref[:, pl.ds(pl.multiple_of(half * wide + h * HD, HD), HD)] = out
        else:
            st_so[:, h * HD:(h + 1) * HD] = out
        x = out.astype(jnp.float32)
        norm = lax.rsqrt(jnp.mean(x * x, axis=1, keepdims=True) + EPS)
        x = (x * norm * gain_ref[...]).astype(jnp.bfloat16)
        query_rows(slot, h, x.astype(jnp.float32))

    def image_level(step):
        away = jnp.where(lax.rem(step, 2) == 0, step // 2, LEVELS - (step + 1) // 2)
        return lax.rem(z + away, LEVELS)

    def advance(step, _):
        @pl.when(step == 1)
        def _():
            forward(1, 2)

        @pl.when(step == 2)
        def _():
            forward(1, 3)
            load(LEVELS // 2 + z)
            attend(both, True, group=z // 2, before=finish_self)
            x_so.start()

        @pl.when(step == 3)
        def _():
            forward(1, 4)

        @pl.when(step == 4)
        def _():
            forward(1, 5)

        @pl.when(step == 5)
        def _():
            forward(1, 6, (0,))

        @pl.when(step == jnp.where(z >= 4, 5, 6))
        def _():
            forward(1, 6, (1,))

        level = image_level(jnp.maximum(step - 2, 0))
        text = jnp.where(step == 1, 1, 0)
        piece = jnp.where(step < 2, text, LEVELS // 2 + level)
        group = jnp.where(step < 2, 4, level // 2)

        @pl.when((step >= 3) | ((step < 2) & (z >= 2 + 2 * step) & ((step == 1) | (z < 6))))
        def _():
            load(piece)
            attend(both, group=group)
        return 0

    lax.fori_loop(0, 7, advance, 0)
    for d in (0, 1):
        await_in(1, d, 4)
        await_in(1, d, 5)

    gate_lane = lax.broadcasted_iota(jnp.int32, gate_ref.shape, 1)

    def finish(turn, _):
        slot = 1 - turn
        tiles = [(slot, h) for h in range(HEADS)]

        def more(step, _):
            level = image_level(step)
            load(LEVELS // 2 + level)
            attend(tiles, group=level // 2)
            return 0

        lax.fori_loop(5, 7, more, 0)

        @pl.when(slot == 1)
        def _():
            x_so.wait_recv()
            self_ref[:, other_wide] = so_in[...]
            for d in (0, 1):
                await_in(1, d, 6)

        level = image_level(7)
        load(LEVELS // 2 + level)
        seen = seen_by(slot, level // 2)
        following = scores_of(tiles[0])
        for h, tile in enumerate(tiles):
            scores = following
            if h + 1 < HEADS:
                following = scores_of(tiles[h + 1])
            _, acc = fold(scores, held(tile), seen)
            gate = jnp.tanh(jnp.sum(
                jnp.where(gate_lane == half * HEADS + h, gate_ref[...], 0.0), axis=1, keepdims=True
            ))
            out = acc[:, :HD] / jnp.maximum(acc[:, HD:], 1.0) * gate
            st_co[slot, :, h * HD:(h + 1) * HD] = out.astype(jnp.bfloat16)
            if h % 2 == 1:
                @pl.when(slot == 1)
                def _():
                    x_co(h // 2).start()
        return 0

    lax.fori_loop(0, 2, finish, 0)
    cross_ref[:, own_wide] = st_co[0]
    for pair in range(HEADS // 2):
        x_co(pair).wait_recv()
    cross_ref[:, other_wide] = co_in[...]

    for copy in (x_self, x_query, x_allow, x_img, x_so):
        copy.wait_send()
    for pair in range(HEADS // 2):
        x_co(pair).wait_send()
    for kind in (0, 1):
        for d in (0, 1):
            for n in range(LAST + 1):
                outgoing(kind, d, n).wait_send()


def per_device(
    queries, keys, values, image_keys, image_values, cross_lo, cross_hi, query_gain, cross_gate
):
    rows, img_rows = queries.shape[0], image_keys.shape[0]
    wide = HEADS * HD
    vmem = pl.BlockSpec(memory_space=pltpu.VMEM)
    bf16, f32 = jnp.bfloat16, jnp.float32
    pin = lambda x: pltpu.with_memory_space_constraint(x, pltpu.HBM)
    return pl.pallas_call(
        kernel,
        out_shape=(jax.ShapeDtypeStruct(queries.shape, bf16),) * 2,
        in_specs=[pl.BlockSpec(memory_space=pltpu.HBM)] * 9,
        out_specs=(vmem, vmem),
        scratch_shapes=[
            pltpu.VMEM((LEVELS // 2 + LEVELS, 4 * rows, 2 * HD), bf16),
            pltpu.VMEM((rows, 2 * HD), bf16),
            pltpu.VMEM((img_rows, 2 * HD), bf16),
            pltpu.VMEM((rows, wide), bf16),
            pltpu.VMEM((rows, HD), bf16),
            pltpu.VMEM((2, HEADS, rows, 2 * HD), bf16),
            pltpu.VMEM((2, HEADS, rows, HD), f32),
            pltpu.VMEM((2, HEADS, rows, 2 * HD), f32),
            pltpu.VMEM((2, 5, rows, HD), f32),
            pltpu.VMEM((rows, wide), bf16),
            pltpu.VMEM((2, rows, wide), bf16),
            pltpu.VMEM((rows, wide), bf16),
            pltpu.VMEM((rows, wide), bf16),
            pltpu.VMEM((4 * rows, 2 * HD), bf16),
            pltpu.VMEM((4 * rows, 2 * HD), bf16),
            pltpu.VMEM((rows, HD), bf16),
            pltpu.VMEM((rows, wide), bf16),
            pltpu.VMEM((rows, wide), bf16),
            pltpu.VMEM((rows // HD, HD), jnp.int32),
            pltpu.VMEM((rows // HD, HD), jnp.int32),
            pltpu.VMEM((1, HD), f32),
            pltpu.VMEM((1, cross_gate.shape[0]), f32),
            pltpu.SemaphoreType.DMA((14,)),
            pltpu.SemaphoreType.DMA((2, 2, LAST + 1)),
            pltpu.SemaphoreType.DMA((2, 2, LAST + 1)),
            pltpu.SemaphoreType.DMA((9,)),
            pltpu.SemaphoreType.DMA((9,)),
        ],
        compiler_params=pltpu.CompilerParams(
            collective_id=0, has_side_effects=True, vmem_limit_bytes=40 * 2**20
        ),
    )(
        *(pin(x) for x in (queries, keys, values, image_keys, image_values)),
        pin(cross_lo.reshape(-1, HD)), pin(cross_hi.reshape(-1, HD)), pin(query_gain[None, :]),
        pin(cross_gate[None, :]),
    )


def solution(mesh):
    split = P(("doc", "ctx"), "head")
    return jax.shard_map(
        per_device,
        mesh=mesh,
        in_specs=(split,) * 5 + (P(("doc", "ctx")), P(("doc", "ctx")), P(), P("head")),
        out_specs=(split, split),
        check_vma=False,
    )
```
